1024 devices in a mesh: node: 32 (over x_lo, y, core), local: 32 (over x_hi, z).
Axes of the slice: x: 8 (x_hi: 4, x_lo: 2; x = x_hi * 2 + x_lo), y: 8, z: 8, core: 2. Of those that a mesh axis runs over, the one named last changes fastest.
Arguments:
- context: bfloat16 [393216, 768], P(('node', 'local')), may hold values from -6 to 6
- cotangent: bfloat16 [393216, 1536], P(('node', 'local')), may hold values from -24 to 24
- weight_codes: bfloat16 [768, 1536], P('local', 'node'), may hold values from -0.21875 to 0.21875
- scales: bfloat16 [768, 32], P('local', 'node'), may hold values from 0.5 to 2
- lengths: int32 [1024], P(('node', 'local')), may hold values from 96 to 384, as said below
Outputs:
- encoded: bfloat16 [393216, 1536], P(('node', 'local'))
- ctx_grad: bfloat16 [393216, 768], P(('node', 'local'))
- weight_grad: float32 [768, 1536], P('local', 'node')
The draws below stay inside these ranges and needn't reach their ends.
Inputs may be any that keep to these rules, and one draw needn't show every extreme that they name: `lengths`: rows of an utterance past its length are padding. Some utterance has all 384 frames in every draw.
All inputs are finite; a program needn't handle non-finite values.
Results may differ from the reference program's by a relative error of at most 0.005.
Values may be sent and summed in bfloat16 or wider, within the bound.
A program may use at most 64 MiB of HBM per device.

```python
import math
import jax
import jax.numpy as jnp
from jax import lax

D = 1536
HROWS = 768
QBLOCK = 48
FRAMES = 384
SAMPLES = 1024
TOKENS = 393216


def draw_lengths(key, part):
    key = jax.random.fold_in(key, 7)
    first_key, second_key = jax.random.split(key)
    drawn = jax.random.randint(first_key, (SAMPLES,), FRAMES // 4, FRAMES + 1)
    chosen = jax.random.randint(second_key, (), 0, SAMPLES)
    return jnp.where(jnp.arange(SAMPLES) == chosen, FRAMES, drawn).astype(jnp.int32)


def with_spikes(values, key, source, target, blocks, factor):
    def block_of(dim):
        return (jnp.arange(values.shape[dim]) // (values.shape[dim] // blocks)).reshape((-1,) + (1,) * (values.ndim - 1 - dim))

    near = jax.random.permutation(key, blocks)[block_of(target)]
    second = (block_of(target) + blocks // 2) % blocks
    return jnp.where((block_of(source) == near) | (block_of(source) == second), factor * values, values)


def steps_of(key, shape, cuts, low, top_value):
    loudness, own = 1.0, jax.random.fold_in(key, 6)
    for dim, shards_of in cuts:
        draws = jnp.exp(jax.random.uniform(jax.random.fold_in(own, dim), (shards_of,), jnp.float32, low / len(cuts), top_value / len(cuts)))
        loudness = loudness * jnp.repeat(draws, shape[dim] // shards_of).reshape([-1 if axis == dim else 1 for axis in range(len(shape))])
    return loudness


def scatter_about(key, shape, spread, limit, shards=(), held_as=jnp.bfloat16):
    loudness = steps_of(key, shape, shards, -0.22, 0.18) if shards else 1.0
    entries = jax.random.normal(key, shape, jnp.float32) * spread * loudness
    return jnp.minimum(jnp.maximum(entries, -limit), limit).astype(held_as)


def noise_with(rng, dims, scale, bound, pieces, heavy, kind=jnp.bfloat16):
    entries = scale * jax.random.normal(rng, dims, jnp.float32)
    if pieces:
        entries = entries * steps_of(rng, dims, pieces, -0.22, 0.18)
    return jnp.clip(with_spikes(entries, jax.random.fold_in(rng, 3), *heavy), -bound, bound).astype(kind)


def setup_inputs(seed: int = 0) -> dict:
    seeds = jax.random.split(jax.random.key(seed), 6)
    return {
        "context": scatter_about(seeds[0], (TOKENS, HROWS), 1.0, 6.0, ((0, 1024),)),
        "cotangent": noise_with(seeds[1], (TOKENS, D), 1.0, 24.0, ((0, 1024),), (0, 1, 512, 6.0)),
        "weight_codes": scatter_about(seeds[2], (HROWS, D), HROWS ** -0.5, 0.21875, ((0, 32), (1, 32))),
        "scales": jnp.clip(jnp.exp(math.log(2.0) - 1.3862944 * jax.random.uniform(seeds[3], (HROWS, D // QBLOCK), jnp.float32) ** steps_of(seeds[3], (HROWS, D // QBLOCK), ((0, 32), (1, 32)), -0.2, 0.2)), 0.5, 2.0).astype(jnp.bfloat16),
        "lengths": draw_lengths(jax.random.fold_in(seeds[5], 71), 0),
    }


def reference(context, cotangent, weight_codes, scales, lengths):
    weight = (weight_codes.astype(jnp.float32).reshape(HROWS, D // QBLOCK, QBLOCK)
              * scales.astype(jnp.float32)[:, :, None]).reshape(HROWS, D).astype(jnp.bfloat16)
    position = jnp.arange(TOKENS, dtype=jnp.int32) % FRAMES
    utterance = jnp.arange(TOKENS, dtype=jnp.int32) // FRAMES
    usable = (position < lengths[utterance])[:, None]
    masked = jnp.where(usable, cotangent, jnp.zeros_like(cotangent))
    product = jnp.dot(context, weight, preferred_element_type=jnp.float32)
    encoded = jnp.where(usable, product, jnp.zeros_like(product)).astype(jnp.bfloat16)
    ctx_grad = lax.dot_general(masked, weight, (((1,), (1,)), ((), ())),
                               preferred_element_type=jnp.float32).astype(jnp.bfloat16)
    weight_grad = lax.dot_general(context, masked, (((0,), (0,)), ((), ())),
                                  preferred_element_type=jnp.float32) / SAMPLES
    return (encoded, ctx_grad, weight_grad)
```

```python
import jax
import jax.numpy as jnp
from jax import lax
from jax.experimental import pallas as pl
from jax.experimental.pallas import tpu as pltpu
from jax.sharding import PartitionSpec as P

MESH = pl.DeviceIdType.MESH
F32, BF16 = jnp.float32, jnp.bfloat16
N = 8
AGQ = 4
RIGHT, LEFT = 0, 1


def kernel(
    context_hbm, cotangent_hbm, codes_ref, scales_ref, lengths_ref,
    encoded_ref, ctx_grad_ref, weight_grad_ref,
    context, cotangent, grad, grad_in, weight, block,
    zsend, zbuf, ypack, ysend, ybuf,
    ring_out, ring_in, rsend, rbuf, xsend, xbuf,
    load_sem, z_s, z_r, y_s, y_r, ag_s, ag_r, fw_s, fw_r,
    pair_s, pair_r, ring_s, ring_r, ry_s, ry_r, rx_s, rx_r,
):
    node, local = lax.axis_index("node"), lax.axis_index("local")
    core, y, x_lo = node % 2, (node // 2) % N, node // (2 * N)
    x_hi, z = local // N, local % N
    x = x_hi * 2 + x_lo

    def at(cx, cy, cz, cc):
        return (((cx % 2) * N + cy) * 2 + cc, (cx // 2) * N + cz)

    def copy(src, dst, send, recv, target):
        return pltpu.make_async_remote_copy(
            src_ref=src, dst_ref=dst, send_sem=send, recv_sem=recv,
            device_id=target, device_id_type=MESH,
        )

    me, mate = at(x, y, z, core), at(x, y, z, 1 - core)

    load_ctx = pltpu.make_async_copy(context_hbm, context, load_sem.at[0])
    load_cot = pltpu.make_async_copy(cotangent_hbm, cotangent, load_sem.at[1])
    load_ctx.start()
    load_cot.start()
    barrier = pltpu.get_barrier_semaphore()

    def greet(target):
        pl.semaphore_signal(barrier, inc=1, device_id=target, device_id_type=MESH)

    greet(mate)
    for k in range(1, N):
        greet(at(x, y, (z + k) % N, core))
        for cc in range(2):
            greet(at(x, (y + k) % N, z, cc))
            greet(at((x + k) % N, y, z, cc))

    own = (codes_ref[...].astype(F32) * scales_ref[...].astype(F32)).astype(BF16)
    zsend[0:24, 0:48] = own

    usable = lax.broadcasted_iota(jnp.int32, (context.shape[0], 1), 0) < lengths_ref[0]
    load_ctx.wait()
    context[...] = jnp.where(usable, context[...], jnp.zeros_like(context))
    load_cot.wait()
    for i in range(2):
        for h in range(2):
            part = lax.dot_general(
                context[:, i * 384 : (i + 1) * 384], cotangent[:, h * 768 : (h + 1) * 768],
                (((0,), (0,)), ((), ())), preferred_element_type=F32,
            )
            grad[h, 2 * i : 2 * i + 2] = part.reshape(2, N, 24, 768)

    pl.semaphore_wait(barrier, 1 + 5 * (N - 1))

    z_copies = [
        copy(zsend, zbuf.at[z], z_s.at[k], z_r.at[z], at(x, y, (z + k) % N, core))
        for k in range(1, N)
    ]
    for c in z_copies:
        c.start()
    zbuf[z] = zsend[...]

    order = (4, 3, 5, 2, 6, 1, 7, 0)
    pair = {}
    for k in order:
        seg = (z + k) % N
        pair[k] = copy(
            grad.at[1 - core, :, seg], grad_in.at[k], pair_s.at[k], pair_r.at[k], mate
        )
        pair[k].start()

    paired = set()

    def own_part(k, q):
        if k not in paired:
            pair[k].wait_recv()
            paired.add(k)
        h, j = q // 2, q % 2
        cols = slice(j * 384, (j + 1) * 384)
        mine = grad[core, 2 * h : 2 * h + 2, (z + k) % N, :, cols]
        return (mine + grad_in[k, 2 * h : 2 * h + 2, :, cols]).reshape(48, 384)

    zn = (at(x, y, (z + 1) % N, core), at(x, y, (z + N - 1) % N, core))
    ring = {}

    def ring_send(way, d, q):
        k = d if way == RIGHT else N - d
        part = own_part(k, q)
        if (way, d + 1, q) in ring:
            ring[way, d + 1, q].wait_recv()
            part = part + ring_in[way, d + 1, q].astype(F32)
        ring_out[way, d, q] = part.astype(BF16)
        c = copy(
            ring_out.at[way, d, q], ring_in.at[way, d, q], ring_s.at[way, d, q],
            ring_r.at[way, d, q], zn[way],
        )
        c.start()
        ring[way, d, q] = c

    def ring_step(d):
        for q in range(4):
            for way in (RIGHT, LEFT):
                if d == 4 and (q < 2) != (way == RIGHT):
                    continue
                ring_send(way, d, q)

    ring_step(4)
    for q in (2, 3):
        ring_send(RIGHT, 3, q)
    for q in (0, 1):
        ring_send(LEFT, 3, q)

    for k in range(1, N):
        s = (z + k) % N
        copy(zbuf.at[s], zbuf.at[s], z_s.at[k], z_r.at[s], me).wait_recv()
    for s in range(N):
        row, lane = (s % 4) * 24, (s // 4) * 64
        ypack[row : row + 24, lane : lane + 48] = zbuf[s, 0:24, 0:48].astype(F32)
    ysend[...] = ypack[...].astype(BF16)
    taker = y // 4
    slot = (y % 4) * 2 + core
    y_copies = [
        copy(ysend, ybuf.at[slot], y_s.at[k], y_r.at[slot], at(x, (y + k) % N, z, taker))
        for k in range(N)
    ]
    for c in y_copies[1:]:
        c.start()

    @pl.when(taker != core)
    def _():
        y_copies[0].start()

    @pl.when(taker == core)
    def _():
        ybuf[slot] = ysend[...]

    for q in (0, 1):
        ring_send(RIGHT, 3, q)
    for q in (2, 3):
        ring_send(LEFT, 3, q)
    ring_step(2)

    for s in range(N):
        @pl.when((4 * core + s // 2 != y) | (core != s % 2))
        def _():
            copy(ybuf.at[s], ybuf.at[s], y_s.at[0], y_r.at[s], me).wait_recv()

        block[0:96, s * 48 : (s + 1) * 48] = ybuf[s, :, 0:48].astype(F32)
        block[96:192, s * 48 : (s + 1) * 48] = ybuf[s, :, 64:112].astype(F32)

    rows = 192 // AGQ

    def place(k, q):
        cx = (x + k) % N
        row = pl.multiple_of((cx // 2) * 192 + q * rows, 16)
        col = pl.multiple_of((cx % 2) * 768 + core * 384, 128)
        return weight.at[pl.ds(row, rows), pl.ds(col, 384)]

    for q in range(AGQ):
        place(0, q)[...] = block[q * rows : (q + 1) * rows, :].astype(BF16)

    xn = (at((x + 1) % N, y, z, core), at((x + N - 1) % N, y, z, core))
    gather, forward = {}, []

    def gather_send(way, s, q):
        if s > 1:
            gather[way, s - 1, q].wait_recv()
        k = 1 - s if way == RIGHT else s - 1
        if s <= 3 or (q < AGQ // 2) == (way == RIGHT):
            spot = place(k + N, q)
            c = copy(spot, spot, ag_s.at[way, s, q], ag_r.at[way, s, q], xn[way])
            c.start()
            gather[way, s, q] = c
        if s > 1 or way == RIGHT:
            share(way, s - 1, q)

    def share(way, s, q):
        k = -s if way == RIGHT else s
        spot = place(k + N, q)
        c = copy(spot, spot, fw_s.at[way, s, q], fw_r.at[way, s, q], mate)
        c.start()
        forward.append((way, s, q))

    def gather_step(s):
        for q in range(AGQ):
            for way in (RIGHT, LEFT):
                gather_send(way, s, q)

    gather_step(1)
    ring_step(1)
    gather_step(2)

    total = []
    for q in range(4):
        a, b = (1, 1)
        ring[RIGHT, a, q].wait_recv()
        ring[LEFT, b, q].wait_recv()
        total.append(
            own_part(0, q) + ring_in[RIGHT, a, q].astype(F32) + ring_in[LEFT, b, q].astype(F32)
        )
    for h in range(2):
        for k in range(N):
            j, lane = k // 4, (k % 4) * 96
            rsend[k, h * 48 : (h + 1) * 48, 0:96] = total[2 * h + j][:, lane : lane + 96].astype(BF16)
    ry_copies = [
        copy(rsend.at[(y + k) % N], rbuf.at[y], ry_s.at[k], ry_r.at[y], at(x, (y + k) % N, z, core))
        for k in range(1, N)
    ]
    for c in ry_copies:
        c.start()

    gather_step(3)

    summed = rsend[y].astype(F32)
    for k in range(1, N):
        s = (y + k) % N
        copy(rbuf.at[s], rbuf.at[s], ry_s.at[k], ry_r.at[s], me).wait_recv()
        summed = summed + rbuf[s].astype(F32)
    for i in range(4):
        for cc in range(2):
            xsend[i, cc, :, 0:48] = summed[i * 24 : (i + 1) * 24, cc * 48 : (cc + 1) * 48]
    rx_copies = []
    for k in range(4):
        for e in range(2):
            i, cc = (x_hi + k) % 4, (core + e) % 2
            rx_copies.append(copy(
                xsend.at[i, cc], xbuf.at[x], rx_s.at[2 * k + e], rx_r.at[x], at(i * 2 + core, y, z, cc)
            ))
    for c in rx_copies[1:]:
        c.start()

    @pl.when(x_lo != core)
    def _():
        rx_copies[0].start()

    @pl.when(x_lo == core)
    def _():
        xbuf[x] = xsend[x_hi, core]

    gather_step(4)
    for q in range(AGQ):
        way = RIGHT if q < AGQ // 2 else LEFT
        gather[way, 4, q].wait_recv()
        share(way, 4, q)

    for k in range(1, N):
        s = (x + k) % N
        copy(xbuf.at[s], xbuf.at[s], rx_s.at[0], rx_r.at[s], me).wait_recv()

    @pl.when(x_lo != core)
    def _():
        copy(xbuf.at[x], xbuf.at[x], rx_s.at[0], rx_r.at[x], me).wait_recv()

    last = xbuf[0]
    for s in range(1, N):
        last = last + xbuf[s]
    weight_grad_ref[...] = last[:, 0:48] * (1.0 / 1024)

    for way, s, q in forward:
        k = -s if way == RIGHT else s
        cx = (x + k + N) % N
        row = pl.multiple_of((cx // 2) * 192 + q * rows, 16)
        col = pl.multiple_of((cx % 2) * 768 + (1 - core) * 384, 128)
        spot = weight.at[pl.ds(row, rows), pl.ds(col, 384)]
        copy(spot, spot, fw_s.at[way, s, q], fw_r.at[way, s, q], mate).wait_recv()

    for j in range(4):
        cols = slice(j * 384, (j + 1) * 384)
        encoded_ref[:, cols] = jnp.dot(
            context[...], weight[:, cols], preferred_element_type=F32
        ).astype(BF16)
    for j in range(2):
        cols = slice(j * 384, (j + 1) * 384)
        product = lax.dot_general(
            cotangent[...], weight[cols, :], (((1,), (1,)), ((), ())), preferred_element_type=F32
        )
        ctx_grad_ref[:, cols] = jnp.where(usable, product, jnp.zeros_like(product)).astype(BF16)

    for c in z_copies + y_copies[1:] + ry_copies + rx_copies[1:]:
        c.wait_send()

    @pl.when(taker != core)
    def _():
        y_copies[0].wait_send()

    @pl.when(x_lo != core)
    def _():
        rx_copies[0].wait_send()

    for c in list(pair.values()) + list(ring.values()) + list(gather.values()):
        c.wait_send()
    for way, s, q in forward:
        spot = place((-s if way == RIGHT else s) + N, q)
        copy(spot, spot, fw_s.at[way, s, q], fw_r.at[way, s, q], mate).wait_send()


def body(context, cotangent, codes, scales, lengths):
    frames, hrows = context.shape
    width = cotangent.shape[1]
    vmem = pl.BlockSpec(memory_space=pltpu.VMEM)
    hbm = pl.BlockSpec(memory_space=pl.ANY)
    dma = pltpu.SemaphoreType.DMA
    return pl.pallas_call(
        kernel,
        out_shape=(
            jax.ShapeDtypeStruct((frames, width), BF16),
            jax.ShapeDtypeStruct((frames, hrows), BF16),
            jax.ShapeDtypeStruct(codes.shape, F32),
        ),
        in_specs=[hbm, hbm, vmem, vmem, pl.BlockSpec(memory_space=pltpu.SMEM)],
        out_specs=(vmem, vmem, vmem),
        scratch_shapes=[
            pltpu.VMEM((frames, hrows), BF16),
            pltpu.VMEM((frames, width), BF16),
            pltpu.VMEM((2, 4, N, 24, width // 2), F32),
            pltpu.VMEM((N, 4, 24, width // 2), F32),
            pltpu.VMEM((hrows, width), BF16),
            pltpu.VMEM((192, 384), F32),
            pltpu.VMEM((32, 128), BF16),
            pltpu.VMEM((N, 32, 128), BF16),
            pltpu.VMEM((96, 128), F32),
            pltpu.VMEM((96, 128), BF16),
            pltpu.VMEM((N, 96, 128), BF16),
            pltpu.VMEM((2, 5, 4, 48, 384), BF16),
            pltpu.VMEM((2, 5, 4, 48, 384), BF16),
            pltpu.VMEM((N, 96, 128), BF16),
            pltpu.VMEM((N, 96, 128), BF16),
            pltpu.VMEM((4, 2, 24, 128), F32),
            pltpu.VMEM((N, 24, 128), F32),
            dma((2,)),
            dma((N,)), dma((N,)),
            dma((N,)), dma((N,)),
            dma((2, 5, AGQ)), dma((2, 5, AGQ)),
            dma((2, 5, AGQ)), dma((2, 5, AGQ)),
            dma((N,)), dma((N,)),
            dma((2, 5, 4)), dma((2, 5, 4)),
            dma((N,)), dma((N,)),
            dma((N,)), dma((N,)),
        ],
        compiler_params=pltpu.CompilerParams(
            collective_id=0, has_side_effects=True, vmem_limit_bytes=48 * 2**20
        ),
    )(context, cotangent, codes, scales, lengths)


def solution(mesh):
    return jax.shard_map(
        body,
        mesh=mesh,
        in_specs=(
            P(("node", "local"), None),
            P(("node", "local"), None),
            P("local", "node"),
            P("local", "node"),
            P(("node", "local")),
        ),
        out_specs=(P(("node", "local"), None), P(("node", "local"), None), P("local", "node")),
        check_vma=False,
    )
```

```python
import jax
import jax.numpy as jnp
from jax import lax
from jax.experimental import pallas as pl
from jax.experimental.pallas import tpu as pltpu
from jax.sharding import PartitionSpec as P

MESH = pl.DeviceIdType.MESH
F32, BF16 = jnp.float32, jnp.bfloat16
N = 8
RIGHT, LEFT = 0, 1
PIECES = 8


FAR = (4, 3, 5, 2, 6, 1, 7)


def kernel(
    context_hbm, cotangent_hbm, codes_hbm, scales_hbm, lengths,
    encoded, ctx_grad, weight_grad,
    context, cotangent, codes, scales, ctx_rows, cot_cols, enc_sum, cg_sum,
    grad, grad_in, weight, block,
    zsend, zbuf, ypack, ysend, ybuf,
    ring_out, ring_in, rsend, rbuf, xsend, xbuf,
    load_sem, z_s, z_r, y_s, y_r, ag_s, ag_r, fw_s, fw_r,
    pair_s, pair_r, ring_s, ring_r, ry_s, ry_r, rx_s, rx_r,
):
    node, local = lax.axis_index("node"), lax.axis_index("local")
    core, y, x_lo = node % 2, (node // 2) % N, node // (2 * N)
    x_hi, z = local // N, local % N
    x = x_hi * 2 + x_lo

    def at(cx, cy, cz, cc):
        return (((cx % 2) * N + cy) * 2 + cc, (cx // 2) * N + cz)

    def copy(src, dst, send, recv, target):
        return pltpu.make_async_remote_copy(
            src_ref=src, dst_ref=dst, send_sem=send, recv_sem=recv,
            device_id=target, device_id_type=MESH,
        )

    me, mate = at(x, y, z, core), at(x, y, z, 1 - core)

    barrier = pltpu.get_barrier_semaphore()

    def greet(target):
        pl.semaphore_signal(barrier, inc=1, device_id=target, device_id_type=MESH)

    for k in FAR:
        greet(at(x, y, (z + k) % N, core))
        for cc in range(2):
            greet(at(x, (y + k) % N, z, cc))
            greet(at((x + k) % N, y, z, cc))
    greet(mate)

    loads = [
        pltpu.make_async_copy(codes_hbm, codes, load_sem.at[2, 0]),
        pltpu.make_async_copy(scales_hbm, scales, load_sem.at[2, 1]),
    ]
    rows = context.shape[0] // PIECES
    for j, (src, dst) in enumerate(((context_hbm, context), (cotangent_hbm, cotangent))):
        for i in range(PIECES):
            spot = slice(i * rows, (i + 1) * rows)
            loads.append(pltpu.make_async_copy(src.at[spot], dst.at[spot], load_sem.at[j, i]))
    for c in loads:
        c.start()

    loads[0].wait()
    loads[1].wait()
    spread = lax.broadcasted_iota(jnp.int32, (24, 24), 0) == lax.broadcasted_iota(jnp.int32, (24, 24), 1)
    scale = jnp.sum(jnp.where(spread, scales[...].astype(F32), 0.0), axis=1, keepdims=True)
    zsend[0:24, 0:48] = (codes[...].astype(F32) * scale).astype(BF16)

    for c in loads[2 : 2 + PIECES]:
        c.wait()
    usable = lax.broadcasted_iota(jnp.int32, (context.shape[0], 1), 0) < lengths[0]
    context[...] = jnp.where(usable, context[...], jnp.zeros_like(context))
    for c in loads[2 + PIECES :]:
        c.wait()
    for h in range(2):
        cols = slice(h * 768, (h + 1) * 768)
        cot_cols[h] = jnp.where(usable, cotangent[:, cols], jnp.zeros((context.shape[0], 768), BF16))
    for i in range(2):
        for h in range(2):
            part = lax.dot_general(
                context[:, i * 384 : (i + 1) * 384], cot_cols[h],
                (((0,), (0,)), ((), ())), preferred_element_type=F32,
            )
            grad[h, 2 * i : 2 * i + 2] = part.reshape(2, N, 24, 768)

    pl.semaphore_wait(barrier, 1 + 5 * (N - 1))

    z_copies = [
        copy(zsend, zbuf.at[z], z_s.at[k], z_r.at[z], at(x, y, (z + k) % N, core)) for k in FAR
    ]
    for c in z_copies:
        c.start()
    zbuf[z] = zsend[...]

    pair = {}
    for k in FAR + (0,):
        pair[k] = copy(
            grad.at[1 - core, :, (z + k) % N], grad_in.at[k], pair_s.at[k], pair_r.at[k], mate
        )
        pair[k].start()

    paired = set()

    def own_part(k, q):
        if k not in paired:
            pair[k].wait_recv()
            paired.add(k)
        h, j = q // 2, q % 2
        cols = slice(j * 384, (j + 1) * 384)
        mine = grad[core, 2 * h : 2 * h + 2, (z + k) % N, :, cols]
        return (mine + grad_in[k, 2 * h : 2 * h + 2, :, cols]).reshape(48, 384)

    zn = (at(x, y, (z + 1) % N, core), at(x, y, (z + N - 1) % N, core))
    ring = {}

    def ring_send(way, d, q):
        part = own_part(d if way == RIGHT else N - d, q)
        if (way, d + 1, q) in ring:
            ring[way, d + 1, q].wait_recv()
            part = part + ring_in[way, d + 1, q].astype(F32)
        ring_out[way, d, q] = part.astype(BF16)
        c = copy(
            ring_out.at[way, d, q], ring_in.at[way, d, q], ring_s.at[way, d, q],
            ring_r.at[way, d, q], zn[way],
        )
        c.start()
        ring[way, d, q] = c

    def ring_long(d):
        for i in range(2):
            ring_send(RIGHT, d, i)
            ring_send(LEFT, d, 2 + i)

    def ring_short(d):
        for i in range(2):
            ring_send(RIGHT, d, 2 + i)
            ring_send(LEFT, d, i)

    ring_long(4)
    ring_short(3)

    for i in range(4):
        ctx_rows[i] = context[:, i * 192 : (i + 1) * 192]
    enc_sum[...] = jnp.zeros_like(enc_sum)
    cg_sum[...] = jnp.zeros_like(cg_sum)

    for k in range(1, N):
        s = (z + k) % N
        copy(zbuf.at[s], zbuf.at[s], z_s.at[k], z_r.at[s], me).wait_recv()
    for s in range(N):
        row, lane = (s % 4) * 24, (s // 4) * 64
        ypack[row : row + 24, lane : lane + 48] = zbuf[s, 0:24, 0:48].astype(F32)
    ysend[...] = ypack[...].astype(BF16)
    taker = y // 4
    slot = (y % 4) * 2 + core

    def y_copy(p, k):
        spot = slice(p * 48, (p + 1) * 48)
        return copy(
            ysend.at[spot], ybuf.at[slot, spot], y_s.at[p, k], y_r.at[p, slot],
            at(x, (y + k) % N, z, taker),
        )

    y_copies = [y_copy(p, k) for p in range(2) for k in FAR]

    @pl.when(taker == core)
    def _():
        ybuf[slot] = ysend[...]

    for p in range(2):
        for c in y_copies[p * 7 : p * 7 + 7]:
            c.start()

        @pl.when(taker != core)
        def _():
            y_copy(p, 0).start()

    ring_long(3)
    ring_short(2)
    ring_long(2)

    def place(k, q, cc):
        cx = (x + k + N) % N
        row = pl.multiple_of((cx // 2) * 192 + q * 48, 16)
        col = pl.multiple_of((cx % 2) * 768 + cc * 384, 128)
        return weight.at[pl.ds(row, 48), pl.ds(col, 384)]

    xn = (at((x + 1) % N, y, z, core), at((x + N - 1) % N, y, z, core))
    gather, forward = {}, []

    def shared(way, s, q, cc):
        spot = place(-s if way == RIGHT else s, q, cc)
        return copy(spot, spot, fw_s.at[way, s, q], fw_r.at[way, s, q], mate)

    def share(way, s, q):
        shared(way, s, q, core).start()
        forward.append((way, s, q))

    def gather_send(s, q):
        for way in (RIGHT, LEFT):
            if s > 1 and (way, s - 1, q) not in gather:
                continue
            if s > 1:
                gather[way, s - 1, q].wait_recv()
            if s <= 3 or (s == 4 and (q < 2) == (way == RIGHT)):
                spot = place(1 - s if way == RIGHT else s - 1, q, core)
                c = copy(spot, spot, ag_s.at[way, s, q], ag_r.at[way, s, q], xn[way])
                c.start()
                gather[way, s, q] = c
        for way in (RIGHT, LEFT):
            if (s == 1 and way == RIGHT) or (s > 1 and (way, s - 1, q) in gather):
                share(way, s - 1, q)

    def products(k, pieces):
        for way, s, q in pieces:
            shared(way, s, q, 1 - core).wait_recv()
        cx = (x + k + N) % N
        row = pl.multiple_of((cx // 2) * 192, 16)
        col = pl.multiple_of((cx % 2) * 768, 128)
        entries = weight[pl.ds(row, 192), pl.ds(col, 768)]
        enc_sum[cx % 2] += jnp.dot(ctx_rows[cx // 2], entries, preferred_element_type=F32)
        cg_sum[cx // 2] += lax.dot_general(
            cot_cols[cx % 2], entries, (((1,), (1,)), ((), ())), preferred_element_type=F32
        )

    def products_at(s):
        if s == 0:
            products(0, [(RIGHT, 0, q) for q in range(4)])
        elif s == 4:
            products(4, [(RIGHT if q < 2 else LEFT, 4, q) for q in range(4)])
        else:
            products(-s, [(RIGHT, s, q) for q in range(4)])
            products(s, [(LEFT, s, q) for q in range(4)])

    def assemble(p):
        spot = slice(p * 48, (p + 1) * 48)
        for s in range(N):
            @pl.when((4 * core + s // 2 != y) | (core != s % 2))
            def _():
                piece = ybuf.at[s, spot]
                copy(piece, piece, y_s.at[p, 0], y_r.at[p, s], me).wait_recv()

            cols = slice(s * 48, (s + 1) * 48)
            block[p * 48 : (p + 1) * 48, cols] = ybuf[s, spot, 0:48].astype(F32)
            block[96 + p * 48 : 96 + (p + 1) * 48, cols] = ybuf[s, spot, 64:112].astype(F32)
        for q in (p, p + 2):
            place(0, q, core)[...] = block[q * 48 : (q + 1) * 48, :].astype(BF16)
            gather_send(1, q)

    assemble(0)
    ring_short(1)
    assemble(1)
    ring_long(1)
    for q in (0, 2):
        gather_send(2, q)
    products_at(0)
    for q in (1, 3):
        gather_send(2, q)

    def ry_copy(h, k):
        spot = slice(h * 48, (h + 1) * 48)
        return copy(
            rsend.at[(y + k) % N, spot], rbuf.at[y, spot], ry_s.at[h, k], ry_r.at[h, y],
            at(x, (y + k) % N, z, core),
        )

    ry_copies = [ry_copy(h, k) for h in range(2) for k in FAR]
    for h in range(2):
        for j in range(2):
            q = 2 * h + j
            ring[RIGHT, 1, q].wait_recv()
            ring[LEFT, 1, q].wait_recv()
            total = own_part(0, q) + ring_in[RIGHT, 1, q].astype(F32) + ring_in[LEFT, 1, q].astype(F32)
            for k in range(4):
                rsend[4 * j + k, h * 48 : (h + 1) * 48, 0:96] = total[:, k * 96 : (k + 1) * 96].astype(BF16)
        for c in ry_copies[h * 7 : h * 7 + 7]:
            c.start()

    for q in (0, 2):
        gather_send(3, q)
    products_at(1)
    for q in (1, 3):
        gather_send(3, q)
    for q in (0, 2):
        gather_send(4, q)

    def rx_copy(i, cc):
        return copy(
            xsend.at[i, cc], xbuf.at[x], rx_s.at[2 * i + cc], rx_r.at[x], at(i * 2 + core, y, z, cc)
        )

    def stays(i, cc):
        return (x_hi == i) & (x_lo == core) & (core == cc)

    for h in range(2):
        spot = slice(h * 48, (h + 1) * 48)
        summed = rsend[y, spot].astype(F32)
        for k in range(1, N):
            s = (y + k) % N
            piece = rbuf.at[s, spot]
            copy(piece, piece, ry_s.at[h, k], ry_r.at[h, s], me).wait_recv()
            summed = summed + rbuf[s, spot].astype(F32)
        for i in range(2):
            for cc in range(2):
                for r in range(3):
                    rows = slice(i * 24 + r * 8, i * 24 + r * 8 + 8)
                    xsend[2 * h + i, cc, :, r * 64 : r * 64 + 48] = summed[rows, cc * 48 : (cc + 1) * 48]
        for i in (2 * h, 2 * h + 1):
            for cc in range(2):
                @pl.when(jnp.logical_not(stays(i, cc)))
                def _():
                    rx_copy(i, cc).start()

                @pl.when(stays(i, cc))
                def _():
                    xbuf[x] = xsend[i, cc]

    for q in (1, 3):
        gather_send(4, q)
    products_at(2)
    for q in range(4):
        gather_send(5, q)
    products_at(3)
    products_at(4)
    for h in range(2):
        encoded[:, h * 768 : (h + 1) * 768] = enc_sum[h].astype(BF16)
    for i in range(4):
        ctx_grad[:, i * 192 : (i + 1) * 192] = cg_sum[i].astype(BF16)

    for k in range(1, N):
        s = (x + k) % N
        copy(xbuf.at[s], xbuf.at[s], rx_s.at[0], rx_r.at[s], me).wait_recv()

    @pl.when(x_lo != core)
    def _():
        copy(xbuf.at[x], xbuf.at[x], rx_s.at[0], rx_r.at[x], me).wait_recv()

    last = xbuf[0]
    for s in range(1, N):
        last = last + xbuf[s]
    for r in range(3):
        weight_grad[r * 8 : r * 8 + 8, :] = last[:, r * 64 : r * 64 + 48] * (1.0 / 1024)

    for c in z_copies + y_copies + ry_copies:
        c.wait_send()

    @pl.when(taker != core)
    def _():
        for p in range(2):
            y_copy(p, 0).wait_send()

    for i in range(4):
        for cc in range(2):
            @pl.when(jnp.logical_not(stays(i, cc)))
            def _():
                rx_copy(i, cc).wait_send()

    for c in list(pair.values()) + list(ring.values()) + list(gather.values()):
        c.wait_send()
    for way, s, q in forward:
        shared(way, s, q, core).wait_send()


def store(encoded, ctx_grad, weight_grad, encoded_hbm, ctx_grad_hbm, weight_grad_hbm, sems):
    copies = [pltpu.make_async_copy(weight_grad, weight_grad_hbm, sems.at[2, 0])]
    rows = encoded.shape[0] // PIECES
    for i in range(PIECES):
        spot = slice(i * rows, (i + 1) * rows)
        copies.append(pltpu.make_async_copy(encoded.at[spot], encoded_hbm.at[spot], sems.at[0, i]))
        copies.append(pltpu.make_async_copy(ctx_grad.at[spot], ctx_grad_hbm.at[spot], sems.at[1, i]))
    for c in copies:
        c.start()
    for c in copies:
        c.wait()


def body(context, cotangent, codes, scales, lengths):
    frames, hrows = context.shape
    width = cotangent.shape[1]
    vmem = pl.BlockSpec(memory_space=pltpu.VMEM)
    hbm = pl.BlockSpec(memory_space=pltpu.HBM)
    dma = pltpu.SemaphoreType.DMA
    shape = jax.ShapeDtypeStruct
    operands = [
        pltpu.with_memory_space_constraint(a, pltpu.HBM)
        for a in (context, cotangent, codes, scales.T)
    ]
    held = pl.pallas_call(
        kernel,
        out_shape=(
            pltpu.VMEM((frames, width), BF16), pltpu.VMEM((frames, hrows), BF16),
            pltpu.VMEM(codes.shape, F32),
        ),
        in_specs=[hbm] * 4 + [pl.BlockSpec(memory_space=pltpu.SMEM)],
        out_specs=(vmem, vmem, vmem),
        scratch_shapes=[
            pltpu.VMEM((frames, hrows), BF16),
            pltpu.VMEM((frames, width), BF16),
            pltpu.VMEM(codes.shape, BF16),
            pltpu.VMEM((1, codes.shape[0]), BF16),
            pltpu.VMEM((4, frames, hrows // 4), BF16),
            pltpu.VMEM((2, frames, width // 2), BF16),
            pltpu.VMEM((2, frames, width // 2), F32),
            pltpu.VMEM((4, frames, hrows // 4), F32),
            pltpu.VMEM((2, 4, N, 24, width // 2), F32),
            pltpu.VMEM((N, 4, 24, width // 2), F32),
            pltpu.VMEM((hrows, width), BF16),
            pltpu.VMEM((192, 384), F32),
            pltpu.VMEM((32, 128), BF16),
            pltpu.VMEM((N, 32, 128), BF16),
            pltpu.VMEM((96, 128), F32),
            pltpu.VMEM((96, 128), BF16),
            pltpu.VMEM((N, 96, 128), BF16),
            pltpu.VMEM((2, 5, 4, 48, 384), BF16),
            pltpu.VMEM((2, 5, 4, 48, 384), BF16),
            pltpu.VMEM((N, 96, 128), BF16),
            pltpu.VMEM((N, 96, 128), BF16),
            pltpu.VMEM((4, 2, 8, 256), F32),
            pltpu.VMEM((N, 8, 256), F32),
            dma((3, PIECES)),
            dma((N,)), dma((N,)),
            dma((2, N)), dma((2, N)),
            dma((2, 5, 4)), dma((2, 5, 4)),
            dma((2, 5, 4)), dma((2, 5, 4)),
            dma((N,)), dma((N,)),
            dma((2, 5, 4)), dma((2, 5, 4)),
            dma((2, N)), dma((2, N)),
            dma((N,)), dma((N,)),
        ],
        compiler_params=pltpu.CompilerParams(
            collective_id=0, has_side_effects=True, vmem_limit_bytes=40 * 2**20
        ),
    )(*operands, lengths)
    return pl.pallas_call(
        store,
        out_shape=(
            shape((frames, width), BF16), shape((frames, hrows), BF16), shape(codes.shape, F32),
        ),
        in_specs=[vmem] * 3,
        out_specs=(hbm,) * 3,
        scratch_shapes=[dma((3, PIECES))],
    )(*(pltpu.with_memory_space_constraint(a, pltpu.VMEM) for a in held))


def solution(mesh):
    return jax.shard_map(
        body,
        mesh=mesh,
        in_specs=(
            P(("node", "local"), None),
            P(("node", "local"), None),
            P("local", "node"),
            P("local", "node"),
            P(("node", "local")),
        ),
        out_specs=(P(("node", "local"), None), P(("node", "local"), None), P("local", "node")),
        check_vma=False,
    )
```

```python
import jax
import jax.numpy as jnp
from jax import lax
from jax.experimental import pallas as pl
from jax.experimental.pallas import tpu as pltpu
from jax.sharding import PartitionSpec as P

MESH = pl.DeviceIdType.MESH
F32, BF16 = jnp.float32, jnp.bfloat16
N = 8
RIGHT, LEFT = 0, 1
PIECES = 8


FAR = (4, 3, 5, 2, 6, 1, 7)


def kernel(
    context_hbm, cotangent_hbm, codes_hbm, scales_hbm, lengths,
    encoded, ctx_grad, weight_grad,
    context, cotangent, codes, scales, ctx_turned, ctx_rows, cot_cols, enc_sum, cg_sum,
    grad, grad_in, weight, block,
    zsend, zbuf, ypack, ysend, ybuf,
    ring_out, ring_in, rsend, rbuf, xsend, xbuf,
    load_sem, z_s, z_r, y_s, y_r, ag_s, ag_r, fw_s, fw_r,
    pair_s, pair_r, ring_s, ring_r, ry_s, ry_r, rx_s, rx_r,
):
    node, local = lax.axis_index("node"), lax.axis_index("local")
    core, y, x_lo = node % 2, (node // 2) % N, node // (2 * N)
    x_hi, z = local // N, local % N
    x = x_hi * 2 + x_lo

    def at(cx, cy, cz, cc):
        return (((cx % 2) * N + cy) * 2 + cc, (cx // 2) * N + cz)

    def copy(src, dst, send, recv, target):
        return pltpu.make_async_remote_copy(
            src_ref=src, dst_ref=dst, send_sem=send, recv_sem=recv,
            device_id=target, device_id_type=MESH,
        )

    me, mate = at(x, y, z, core), at(x, y, z, 1 - core)

    barrier = pltpu.get_barrier_semaphore()

    def greet(target):
        pl.semaphore_signal(barrier, inc=1, device_id=target, device_id_type=MESH)

    for k in FAR:
        greet(at(x, y, (z + k) % N, core))
        for cc in range(2):
            greet(at(x, (y + k) % N, z, cc))
            greet(at((x + k) % N, y, z, cc))
    greet(mate)

    loads = [
        pltpu.make_async_copy(codes_hbm, codes, load_sem.at[2, 0]),
        pltpu.make_async_copy(scales_hbm, scales, load_sem.at[2, 1]),
    ]
    rows = context.shape[0] // PIECES
    for j, (src, dst) in enumerate(((context_hbm, context), (cotangent_hbm, cotangent))):
        for i in range(PIECES):
            spot = slice(i * rows, (i + 1) * rows)
            loads.append(pltpu.make_async_copy(src.at[spot], dst.at[spot], load_sem.at[j, i]))
    for c in loads:
        c.start()

    loads[0].wait()
    loads[1].wait()
    spread = lax.broadcasted_iota(jnp.int32, (24, 24), 0) == lax.broadcasted_iota(jnp.int32, (24, 24), 1)
    scale = jnp.sum(jnp.where(spread, scales[...].astype(F32), 0.0), axis=1, keepdims=True)
    zsend[0:24, 0:48] = (codes[...].astype(F32) * scale).astype(BF16)

    for c in loads[2 : 2 + PIECES]:
        c.wait()
    usable = lax.broadcasted_iota(jnp.int32, (context.shape[0], 1), 0) < lengths[0]
    context[...] = jnp.where(usable, context[...], jnp.zeros_like(context))
    ctx_turned[...] = context[...].T

    for c in loads[2 + PIECES :]:
        c.wait()

    def own_gradient(h):
        entries = cotangent[:, pl.ds(pl.multiple_of(h * 768, 128), 768)]
        for i in range(2):
            part = jnp.dot(ctx_turned[i * 384 : (i + 1) * 384], entries, preferred_element_type=F32)
            grad[h, 2 * i : 2 * i + 2] = part.reshape(2, N, 24, 768)

    own_gradient(1 - core)
    pl.semaphore_wait(barrier, 1 + 5 * (N - 1))

    z_copies = [
        copy(zsend, zbuf.at[z], z_s.at[k], z_r.at[z], at(x, y, (z + k) % N, core)) for k in FAR
    ]
    for c in z_copies:
        c.start()
    zbuf[z] = zsend[...]

    pair = {}
    for k in FAR + (0,):
        pair[k] = copy(
            grad.at[1 - core, :, (z + k) % N], grad_in.at[k], pair_s.at[k], pair_r.at[k], mate
        )
        pair[k].start()
    own_gradient(core)

    paired = set()

    def own_part(k, q):
        if k not in paired:
            pair[k].wait_recv()
            paired.add(k)
        h, j = q // 2, q % 2
        cols = slice(j * 384, (j + 1) * 384)
        mine = grad[core, 2 * h : 2 * h + 2, (z + k) % N, :, cols]
        return (mine + grad_in[k, 2 * h : 2 * h + 2, :, cols]).reshape(48, 384)

    zn = (at(x, y, (z + 1) % N, core), at(x, y, (z + N - 1) % N, core))
    ring = {}

    def ring_send(way, d, q):
        part = own_part(d if way == RIGHT else N - d, q)
        if (way, d + 1, q) in ring:
            ring[way, d + 1, q].wait_recv()
            part = part + ring_in[way, d + 1, q].astype(F32)
        ring_out[way, d, q] = part.astype(BF16)
        c = copy(
            ring_out.at[way, d, q], ring_in.at[way, d, q], ring_s.at[way, d, q],
            ring_r.at[way, d, q], zn[way],
        )
        c.start()
        ring[way, d, q] = c

    def ring_long(d):
        for i in range(2):
            ring_send(RIGHT, d, i)
            ring_send(LEFT, d, 2 + i)

    def ring_short(d):
        for i in range(2):
            ring_send(RIGHT, d, 2 + i)
            ring_send(LEFT, d, i)

    taker = y // 4
    slot = (y % 4) * 2 + core

    def y_copy(p, k):
        spot = slice(p * 48, (p + 1) * 48)
        return copy(
            ysend.at[spot], ybuf.at[slot, spot], y_s.at[p, k], y_r.at[p, slot],
            at(x, (y + k) % N, z, taker),
        )

    y_copies = [y_copy(p, k) for p in range(2) for k in FAR]

    def weight_rows():
        for k in range(1, N):
            s = (z + k) % N
            copy(zbuf.at[s], zbuf.at[s], z_s.at[k], z_r.at[s], me).wait_recv()
        for s in range(N):
            row, lane = (s % 4) * 24, (s // 4) * 64
            ypack[row : row + 24, lane : lane + 48] = zbuf[s, 0:24, 0:48].astype(F32)
        ysend[...] = ypack[...].astype(BF16)

        @pl.when(taker == core)
        def _():
            ybuf[slot] = ysend[...]

        for p in range(2):
            for c in y_copies[p * 7 : p * 7 + 7]:
                c.start()

            @pl.when(taker != core)
            def _():
                y_copy(p, 0).start()

    def prepare():
        for i in range(4):
            ctx_rows[i] = context[:, i * 192 : (i + 1) * 192]
        for h in range(2):
            cols = slice(h * 768, (h + 1) * 768)
            cot_cols[h] = jnp.where(usable, cotangent[:, cols], jnp.zeros((context.shape[0], 768), BF16))
        enc_sum[...] = jnp.zeros_like(enc_sum)
        cg_sum[...] = jnp.zeros_like(cg_sum)

    def place(k, q, cc):
        cx = (x + k + N) % N
        row = pl.multiple_of((cx // 2) * 192 + q * 48, 16)
        col = pl.multiple_of((cx % 2) * 768 + cc * 384, 128)
        return weight.at[pl.ds(row, 48), pl.ds(col, 384)]

    xn = (at((x + 1) % N, y, z, core), at((x + N - 1) % N, y, z, core))
    gather, forward = {}, []

    def shared(way, s, q, cc):
        spot = place(-s if way == RIGHT else s, q, cc)
        return copy(spot, spot, fw_s.at[way, s, q], fw_r.at[way, s, q], mate)

    def share(way, s, q):
        shared(way, s, q, core).start()
        forward.append((way, s, q))

    def gather_send(s, q):
        for way in (RIGHT, LEFT):
            if s > 1 and (way, s - 1, q) not in gather:
                continue
            if s > 1:
                gather[way, s - 1, q].wait_recv()
            if s <= 3 or (s == 4 and (q < 2) == (way == RIGHT)):
                spot = place(1 - s if way == RIGHT else s - 1, q, core)
                c = copy(spot, spot, ag_s.at[way, s, q], ag_r.at[way, s, q], xn[way])
                c.start()
                gather[way, s, q] = c
        for way in (RIGHT, LEFT):
            if (s == 1 and way == RIGHT) or (s > 1 and (way, s - 1, q) in gather):
                share(way, s - 1, q)

    def products(k, pieces):
        for way, s, q in pieces:
            shared(way, s, q, 1 - core).wait_recv()
        cx = (x + k + N) % N
        row = pl.multiple_of((cx // 2) * 192, 16)
        col = pl.multiple_of((cx % 2) * 768, 128)
        entries = weight[pl.ds(row, 192), pl.ds(col, 768)]
        enc_sum[cx % 2] += jnp.dot(ctx_rows[cx // 2], entries, preferred_element_type=F32)
        cg_sum[cx // 2] += lax.dot_general(
            cot_cols[cx % 2], entries, (((1,), (1,)), ((), ())), preferred_element_type=F32
        )

    def products_at(s):
        if s == 0:
            products(0, [(RIGHT, 0, q) for q in range(4)])
        elif s == 4:
            products(4, [(RIGHT if q < 2 else LEFT, 4, q) for q in range(4)])
        else:
            products(-s, [(RIGHT, s, q) for q in range(4)])
            products(s, [(LEFT, s, q) for q in range(4)])

    def assemble(p):
        spot = slice(p * 48, (p + 1) * 48)
        for s in range(N):
            @pl.when((4 * core + s // 2 != y) | (core != s % 2))
            def _():
                piece = ybuf.at[s, spot]
                copy(piece, piece, y_s.at[p, 0], y_r.at[p, s], me).wait_recv()

            cols = slice(s * 48, (s + 1) * 48)
            block[p * 48 : (p + 1) * 48, cols] = ybuf[s, spot, 0:48].astype(F32)
            block[96 + p * 48 : 96 + (p + 1) * 48, cols] = ybuf[s, spot, 64:112].astype(F32)
        for q in (p, p + 2):
            place(0, q, core)[...] = block[q * 48 : (q + 1) * 48, :].astype(BF16)
            gather_send(1, q)

    def gather_both(s, first):
        for q in (first, first + 2):
            gather_send(s, q)

    def ry_copy(h, k):
        spot = slice(h * 48, (h + 1) * 48)
        return copy(
            rsend.at[(y + k) % N, spot], rbuf.at[y, spot], ry_s.at[h, k], ry_r.at[h, y],
            at(x, (y + k) % N, z, core),
        )

    ry_copies = [ry_copy(h, k) for h in range(2) for k in FAR]
    def segment(h):
        for j in range(2):
            q = 2 * h + j
            ring[RIGHT, 1, q].wait_recv()
            ring[LEFT, 1, q].wait_recv()
            total = own_part(0, q) + ring_in[RIGHT, 1, q].astype(F32) + ring_in[LEFT, 1, q].astype(F32)
            for k in range(4):
                rsend[4 * j + k, h * 48 : (h + 1) * 48, 0:96] = total[:, k * 96 : (k + 1) * 96].astype(BF16)
        for c in ry_copies[h * 7 : h * 7 + 7]:
            c.start()

    def rx_copy(i, cc):
        return copy(
            xsend.at[i, cc], xbuf.at[x], rx_s.at[2 * i + cc], rx_r.at[x], at(i * 2 + core, y, z, cc)
        )

    def stays(i, cc):
        return (x_hi == i) & (x_lo == core) & (core == cc)

    def summed_over_y(h):
        spot = slice(h * 48, (h + 1) * 48)
        summed = rsend[y, spot].astype(F32)
        for k in range(1, N):
            s = (y + k) % N
            piece = rbuf.at[s, spot]
            copy(piece, piece, ry_s.at[h, k], ry_r.at[h, s], me).wait_recv()
            summed = summed + rbuf[s, spot].astype(F32)
        for i in range(2):
            for cc in range(2):
                for r in range(3):
                    rows = slice(i * 24 + r * 8, i * 24 + r * 8 + 8)
                    xsend[2 * h + i, cc, :, r * 64 : r * 64 + 48] = summed[rows, cc * 48 : (cc + 1) * 48]
        for i in (2 * h, 2 * h + 1):
            for cc in range(2):
                @pl.when(jnp.logical_not(stays(i, cc)))
                def _():
                    rx_copy(i, cc).start()

                @pl.when(stays(i, cc))
                def _():
                    xbuf[x] = xsend[i, cc]

    def finish(far):
        half = x_lo if far else 1 - x_lo
        col = pl.multiple_of(half * 768, 128)
        encoded[:, pl.ds(col, 768)] = enc_sum[half].astype(BF16)
        if far:
            for i in range(4):
                ctx_grad[:, i * 192 : (i + 1) * 192] = cg_sum[i].astype(BF16)

    ring_long(4)
    ring_short(3)
    prepare()
    weight_rows()
    ring_long(3)
    ring_short(2)
    ring_long(2)
    assemble(0)
    ring_short(1)
    assemble(1)
    ring_long(1)
    gather_both(2, 0)
    products_at(0)
    segment(0)
    segment(1)
    gather_both(2, 1)
    gather_both(3, 0)
    products_at(1)
    gather_both(3, 1)
    gather_both(4, 0)
    summed_over_y(0)
    summed_over_y(1)
    gather_both(4, 1)
    products_at(2)
    products_at(3)
    finish(False)
    gather_both(5, 0)
    gather_both(5, 1)
    products_at(4)
    finish(True)


    for k in range(1, N):
        s = (x + k) % N
        copy(xbuf.at[s], xbuf.at[s], rx_s.at[0], rx_r.at[s], me).wait_recv()

    @pl.when(x_lo != core)
    def _():
        copy(xbuf.at[x], xbuf.at[x], rx_s.at[0], rx_r.at[x], me).wait_recv()

    last = xbuf[0]
    for s in range(1, N):
        last = last + xbuf[s]
    for r in range(3):
        weight_grad[r * 8 : r * 8 + 8, :] = last[:, r * 64 : r * 64 + 48] * (1.0 / 1024)

    for c in z_copies + y_copies + ry_copies:
        c.wait_send()

    @pl.when(taker != core)
    def _():
        for p in range(2):
            y_copy(p, 0).wait_send()

    for i in range(4):
        for cc in range(2):
            @pl.when(jnp.logical_not(stays(i, cc)))
            def _():
                rx_copy(i, cc).wait_send()

    for c in list(pair.values()) + list(ring.values()) + list(gather.values()):
        c.wait_send()
    for way, s, q in forward:
        shared(way, s, q, core).wait_send()


def store(encoded, ctx_grad, weight_grad, encoded_hbm, ctx_grad_hbm, weight_grad_hbm, sems):
    copies = [pltpu.make_async_copy(weight_grad, weight_grad_hbm, sems.at[2, 0])]
    rows = encoded.shape[0] // PIECES
    for i in range(PIECES):
        spot = slice(i * rows, (i + 1) * rows)
        copies.append(pltpu.make_async_copy(encoded.at[spot], encoded_hbm.at[spot], sems.at[0, i]))
        copies.append(pltpu.make_async_copy(ctx_grad.at[spot], ctx_grad_hbm.at[spot], sems.at[1, i]))
    for c in copies:
        c.start()
    for c in copies:
        c.wait()


def body(context, cotangent, codes, scales, lengths):
    frames, hrows = context.shape
    width = cotangent.shape[1]
    vmem = pl.BlockSpec(memory_space=pltpu.VMEM)
    hbm = pl.BlockSpec(memory_space=pltpu.HBM)
    dma = pltpu.SemaphoreType.DMA
    shape = jax.ShapeDtypeStruct
    operands = [
        pltpu.with_memory_space_constraint(a, pltpu.HBM)
        for a in (context, cotangent, codes, scales.T)
    ]
    held = pl.pallas_call(
        kernel,
        out_shape=(
            pltpu.VMEM((frames, width), BF16), pltpu.VMEM((frames, hrows), BF16),
            pltpu.VMEM(codes.shape, F32),
        ),
        in_specs=[hbm] * 4 + [pl.BlockSpec(memory_space=pltpu.SMEM)],
        out_specs=(vmem, vmem, vmem),
        scratch_shapes=[
            pltpu.VMEM((frames, hrows), BF16),
            pltpu.VMEM((frames, width), BF16),
            pltpu.VMEM(codes.shape, BF16),
            pltpu.VMEM((1, codes.shape[0]), BF16),
            pltpu.VMEM((hrows, frames), BF16),
            pltpu.VMEM((4, frames, hrows // 4), BF16),
            pltpu.VMEM((2, frames, width // 2), BF16),
            pltpu.VMEM((2, frames, width // 2), F32),
            pltpu.VMEM((4, frames, hrows // 4), F32),
            pltpu.VMEM((2, 4, N, 24, width // 2), F32),
            pltpu.VMEM((N, 4, 24, width // 2), F32),
            pltpu.VMEM((hrows, width), BF16),
            pltpu.VMEM((192, 384), F32),
            pltpu.VMEM((32, 128), BF16),
            pltpu.VMEM((N, 32, 128), BF16),
            pltpu.VMEM((96, 128), F32),
            pltpu.VMEM((96, 128), BF16),
            pltpu.VMEM((N, 96, 128), BF16),
            pltpu.VMEM((2, 5, 4, 48, 384), BF16),
            pltpu.VMEM((2, 5, 4, 48, 384), BF16),
            pltpu.VMEM((N, 96, 128), BF16),
            pltpu.VMEM((N, 96, 128), BF16),
            pltpu.VMEM((4, 2, 8, 256), F32),
            pltpu.VMEM((N, 8, 256), F32),
            dma((3, PIECES)),
            dma((N,)), dma((N,)),
            dma((2, N)), dma((2, N)),
            dma((2, 5, 4)), dma((2, 5, 4)),
            dma((2, 5, 4)), dma((2, 5, 4)),
            dma((N,)), dma((N,)),
            dma((2, 5, 4)), dma((2, 5, 4)),
            dma((2, N)), dma((2, N)),
            dma((N,)), dma((N,)),
        ],
        compiler_params=pltpu.CompilerParams(
            collective_id=0, has_side_effects=True, vmem_limit_bytes=40 * 2**20
        ),
    )(*operands, lengths)
    return pl.pallas_call(
        store,
        out_shape=(
            shape((frames, width), BF16), shape((frames, hrows), BF16), shape(codes.shape, F32),
        ),
        in_specs=[vmem] * 3,
        out_specs=(hbm,) * 3,
        scratch_shapes=[dma((3, PIECES))],
    )(*(pltpu.with_memory_space_constraint(a, pltpu.VMEM) for a in held))


def solution(mesh):
    return jax.shard_map(
        body,
        mesh=mesh,
        in_specs=(
            P(("node", "local"), None),
            P(("node", "local"), None),
            P("local", "node"),
            P("local", "node"),
            P(("node", "local")),
        ),
        out_specs=(P(("node", "local"), None), P(("node", "local"), None), P("local", "node")),
        check_vma=False,
    )
```

```python
import jax
import jax.numpy as jnp
from jax import lax
from jax.experimental import pallas as pl
from jax.experimental.pallas import tpu as pltpu
from jax.sharding import PartitionSpec as P

MESH = pl.DeviceIdType.MESH
F32, BF16 = jnp.float32, jnp.bfloat16
N = 8
RIGHT, LEFT = 0, 1
PIECES = 8


FAR = (4, 3, 5, 2, 6, 1, 7)


def kernel(
    context_hbm, cotangent_hbm, codes_hbm, scales_hbm, lengths_hbm,
    encoded, ctx_grad, weight_grad,
    context, cotangent, codes, scales, lengths, ctx_turned, ctx_rows, cot_cols, enc_sum, cg_sum,
    grad, grad_in, weight, block,
    zsend, zbuf, ypack, ysend, ybuf,
    ring_out, ring_in, rsend, rbuf, xsend, xbuf,
    load_sem, z_s, z_r, y_s, y_r, ag_s, ag_r, fw_s, fw_r,
    pair_s, pair_r, ring_s, ring_r, ry_s, ry_r, rx_s, rx_r,
):
    node, local = lax.axis_index("node"), lax.axis_index("local")
    core, y, x_lo = node % 2, (node // 2) % N, node // (2 * N)
    x_hi, z = local // N, local % N
    x = x_hi * 2 + x_lo

    def at(cx, cy, cz, cc):
        return (((cx % 2) * N + cy) * 2 + cc, (cx // 2) * N + cz)

    def copy(src, dst, send, recv, target):
        return pltpu.make_async_remote_copy(
            src_ref=src, dst_ref=dst, send_sem=send, recv_sem=recv,
            device_id=target, device_id_type=MESH,
        )

    me, mate = at(x, y, z, core), at(x, y, z, 1 - core)

    barrier = pltpu.get_barrier_semaphore()

    def greet(target):
        pl.semaphore_signal(barrier, inc=1, device_id=target, device_id_type=MESH)

    for k in FAR:
        greet(at(x, y, (z + k) % N, core))
        for cc in range(2):
            greet(at(x, (y + k) % N, z, cc))
            greet(at((x + k) % N, y, z, cc))
    greet(mate)

    loads = [
        pltpu.make_async_copy(codes_hbm, codes, load_sem.at[2, 0]),
        pltpu.make_async_copy(scales_hbm, scales, load_sem.at[2, 1]),
        pltpu.make_async_copy(lengths_hbm, lengths, load_sem.at[2, 2]),
    ]
    rows = context.shape[0] // PIECES
    for j, (src, dst) in enumerate(((context_hbm, context), (cotangent_hbm, cotangent))):
        for i in range(PIECES):
            spot = slice(i * rows, (i + 1) * rows)
            loads.append(pltpu.make_async_copy(src.at[spot], dst.at[spot], load_sem.at[j, i]))
    for c in loads:
        c.start()

    loads[0].wait()
    loads[1].wait()
    spread = lax.broadcasted_iota(jnp.int32, (24, 24), 0) == lax.broadcasted_iota(jnp.int32, (24, 24), 1)
    scale = jnp.sum(jnp.where(spread, scales[...].astype(F32), 0.0), axis=1, keepdims=True)
    zsend[0:24, 0:48] = (codes[...].astype(F32) * scale).astype(BF16)

    for c in loads[2 : 3 + PIECES]:
        c.wait()
    usable = lax.broadcasted_iota(jnp.int32, (context.shape[0], 1), 0) < lengths[0, 0]
    context[...] = jnp.where(usable, context[...], jnp.zeros_like(context))
    ctx_turned[...] = context[...].T

    for c in loads[3 + PIECES :]:
        c.wait()

    def own_gradient(h):
        entries = cotangent[:, pl.ds(pl.multiple_of(h * 768, 128), 768)]
        for i in range(2):
            part = jnp.dot(ctx_turned[i * 384 : (i + 1) * 384], entries, preferred_element_type=F32)
            grad[h, 2 * i : 2 * i + 2] = part.reshape(2, N, 24, 768)

    own_gradient(1 - core)
    pl.semaphore_wait(barrier, 1 + 5 * (N - 1))

    z_copies = [
        copy(zsend, zbuf.at[z], z_s.at[k], z_r.at[z], at(x, y, (z + k) % N, core)) for k in FAR
    ]
    for c in z_copies:
        c.start()
    zbuf[z] = zsend[...]

    pair = {}
    for k in FAR + (0,):
        pair[k] = copy(
            grad.at[1 - core, :, (z + k) % N], grad_in.at[k], pair_s.at[k], pair_r.at[k], mate
        )
        pair[k].start()
    own_gradient(core)

    paired = set()

    def own_part(k, q):
        if k not in paired:
            pair[k].wait_recv()
            paired.add(k)
        h, j = q // 2, q % 2
        cols = slice(j * 384, (j + 1) * 384)
        mine = grad[core, 2 * h : 2 * h + 2, (z + k) % N, :, cols]
        return (mine + grad_in[k, 2 * h : 2 * h + 2, :, cols]).reshape(48, 384)

    zn = (at(x, y, (z + 1) % N, core), at(x, y, (z + N - 1) % N, core))
    ring = {}

    def ring_send(way, d, q):
        part = own_part(d if way == RIGHT else N - d, q)
        if (way, d + 1, q) in ring:
            ring[way, d + 1, q].wait_recv()
            part = part + ring_in[way, d + 1, q].astype(F32)
        ring_out[way, d, q] = part.astype(BF16)
        c = copy(
            ring_out.at[way, d, q], ring_in.at[way, d, q], ring_s.at[way, d, q],
            ring_r.at[way, d, q], zn[way],
        )
        c.start()
        ring[way, d, q] = c

    def ring_long(d):
        for i in range(2):
            ring_send(RIGHT, d, i)
            ring_send(LEFT, d, 2 + i)

    def ring_short(d):
        for i in range(2):
            ring_send(RIGHT, d, 2 + i)
            ring_send(LEFT, d, i)

    taker = y // 4
    slot = (y % 4) * 2 + core

    def y_copy(p, k):
        spot = slice(p * 48, (p + 1) * 48)
        return copy(
            ysend.at[spot], ybuf.at[slot, spot], y_s.at[p, k], y_r.at[p, slot],
            at(x, (y + k) % N, z, taker),
        )

    y_copies = [y_copy(p, k) for p in range(2) for k in FAR]

    def weight_rows():
        for k in range(1, N):
            s = (z + k) % N
            copy(zbuf.at[s], zbuf.at[s], z_s.at[k], z_r.at[s], me).wait_recv()
        for s in range(N):
            row, lane = (s % 4) * 24, (s // 4) * 64
            ypack[row : row + 24, lane : lane + 48] = zbuf[s, 0:24, 0:48].astype(F32)
        ysend[...] = ypack[...].astype(BF16)

        @pl.when(taker == core)
        def _():
            ybuf[slot] = ysend[...]

        for p in range(2):
            for c in y_copies[p * 7 : p * 7 + 7]:
                c.start()

            @pl.when(taker != core)
            def _():
                y_copy(p, 0).start()

    def prepare():
        for i in range(4):
            ctx_rows[i] = context[:, i * 192 : (i + 1) * 192]
        for h in range(2):
            cols = slice(h * 768, (h + 1) * 768)
            cot_cols[h] = jnp.where(usable, cotangent[:, cols], jnp.zeros((context.shape[0], 768), BF16))
        enc_sum[...] = jnp.zeros_like(enc_sum)
        cg_sum[...] = jnp.zeros_like(cg_sum)

    def place(k, q, cc):
        cx = (x + k + N) % N
        row = pl.multiple_of((cx // 2) * 192 + q * 48, 16)
        col = pl.multiple_of((cx % 2) * 768 + cc * 384, 128)
        return weight.at[pl.ds(row, 48), pl.ds(col, 384)]

    xn = (at((x + 1) % N, y, z, core), at((x + N - 1) % N, y, z, core))
    gather, forward = {}, []

    def shared(way, s, q, cc):
        spot = place(-s if way == RIGHT else s, q, cc)
        return copy(spot, spot, fw_s.at[way, s, q], fw_r.at[way, s, q], mate)

    def share(way, s, q):
        shared(way, s, q, core).start()
        forward.append((way, s, q))

    def gather_send(s, q):
        for way in (RIGHT, LEFT):
            if s > 1 and (way, s - 1, q) not in gather:
                continue
            if s > 1:
                gather[way, s - 1, q].wait_recv()
            if s <= 3 or (s == 4 and (q < 2) == (way == RIGHT)):
                spot = place(1 - s if way == RIGHT else s - 1, q, core)
                c = copy(spot, spot, ag_s.at[way, s, q], ag_r.at[way, s, q], xn[way])
                c.start()
                gather[way, s, q] = c
        for way in (RIGHT, LEFT):
            if (s == 1 and way == RIGHT) or (s > 1 and (way, s - 1, q) in gather):
                share(way, s - 1, q)

    def products(k, pieces):
        for way, s, q in pieces:
            shared(way, s, q, 1 - core).wait_recv()
        cx = (x + k + N) % N
        row = pl.multiple_of((cx // 2) * 192, 16)
        col = pl.multiple_of((cx % 2) * 768, 128)
        entries = weight[pl.ds(row, 192), pl.ds(col, 768)]
        enc_sum[cx % 2] += jnp.dot(ctx_rows[cx // 2], entries, preferred_element_type=F32)
        cg_sum[cx // 2] += lax.dot_general(
            cot_cols[cx % 2], entries, (((1,), (1,)), ((), ())), preferred_element_type=F32
        )

    def products_at(s):
        if s == 0:
            products(0, [(RIGHT, 0, q) for q in range(4)])
        elif s == 4:
            products(4, [(RIGHT if q < 2 else LEFT, 4, q) for q in range(4)])
        else:
            products(-s, [(RIGHT, s, q) for q in range(4)])
            products(s, [(LEFT, s, q) for q in range(4)])

    def assemble(p):
        spot = slice(p * 48, (p + 1) * 48)
        for s in range(N):
            @pl.when((4 * core + s // 2 != y) | (core != s % 2))
            def _():
                piece = ybuf.at[s, spot]
                copy(piece, piece, y_s.at[p, 0], y_r.at[p, s], me).wait_recv()

            cols = slice(s * 48, (s + 1) * 48)
            block[p * 48 : (p + 1) * 48, cols] = ybuf[s, spot, 0:48].astype(F32)
            block[96 + p * 48 : 96 + (p + 1) * 48, cols] = ybuf[s, spot, 64:112].astype(F32)
        for q in (p, p + 2):
            place(0, q, core)[...] = block[q * 48 : (q + 1) * 48, :].astype(BF16)
            gather_send(1, q)

    def gather_both(s, first):
        for q in (first, first + 2):
            gather_send(s, q)

    def ry_copy(h, k):
        spot = slice(h * 48, (h + 1) * 48)
        return copy(
            rsend.at[(y + k) % N, spot], rbuf.at[y, spot], ry_s.at[h, k], ry_r.at[h, y],
            at(x, (y + k) % N, z, core),
        )

    ry_copies = [ry_copy(h, k) for h in range(2) for k in FAR]
    def segment(h):
        for j in range(2):
            q = 2 * h + j
            ring[RIGHT, 1, q].wait_recv()
            ring[LEFT, 1, q].wait_recv()
            total = own_part(0, q) + ring_in[RIGHT, 1, q].astype(F32) + ring_in[LEFT, 1, q].astype(F32)
            for k in range(4):
                rsend[4 * j + k, h * 48 : (h + 1) * 48, 0:96] = total[:, k * 96 : (k + 1) * 96].astype(BF16)
        for c in ry_copies[h * 7 : h * 7 + 7]:
            c.start()

    def rx_copy(i, cc):
        return copy(
            xsend.at[i, cc], xbuf.at[x], rx_s.at[2 * i + cc], rx_r.at[x], at(i * 2 + core, y, z, cc)
        )

    def stays(i, cc):
        return (x_hi == i) & (x_lo == core) & (core == cc)

    def summed_over_y(h):
        spot = slice(h * 48, (h + 1) * 48)
        summed = rsend[y, spot].astype(F32)
        for k in range(1, N):
            s = (y + k) % N
            piece = rbuf.at[s, spot]
            copy(piece, piece, ry_s.at[h, k], ry_r.at[h, s], me).wait_recv()
            summed = summed + rbuf[s, spot].astype(F32)
        for i in range(2):
            for cc in range(2):
                for r in range(3):
                    rows = slice(i * 24 + r * 8, i * 24 + r * 8 + 8)
                    xsend[2 * h + i, cc, :, r * 64 : r * 64 + 48] = summed[rows, cc * 48 : (cc + 1) * 48]
        for i in (2 * h, 2 * h + 1):
            for cc in range(2):
                @pl.when(jnp.logical_not(stays(i, cc)))
                def _():
                    rx_copy(i, cc).start()

                @pl.when(stays(i, cc))
                def _():
                    xbuf[x] = xsend[i, cc]

    def finish(far):
        half = x_lo if far else 1 - x_lo
        col = pl.multiple_of(half * 768, 128)
        encoded[:, pl.ds(col, 768)] = enc_sum[half].astype(BF16)
        if far:
            for i in range(4):
                ctx_grad[:, i * 192 : (i + 1) * 192] = cg_sum[i].astype(BF16)

    ring_long(4)
    ring_short(3)
    prepare()
    weight_rows()
    ring_long(3)
    ring_short(2)
    ring_long(2)
    assemble(0)
    ring_short(1)
    assemble(1)
    ring_long(1)
    gather_both(2, 0)
    products_at(0)
    segment(0)
    segment(1)
    gather_both(2, 1)
    gather_both(3, 0)
    products_at(1)
    gather_both(3, 1)
    gather_both(4, 0)
    summed_over_y(0)
    summed_over_y(1)
    gather_both(4, 1)
    products_at(2)
    products_at(3)
    finish(False)
    gather_both(5, 0)
    gather_both(5, 1)
    products_at(4)
    finish(True)


    for k in range(1, N):
        s = (x + k) % N
        copy(xbuf.at[s], xbuf.at[s], rx_s.at[0], rx_r.at[s], me).wait_recv()

    @pl.when(x_lo != core)
    def _():
        copy(xbuf.at[x], xbuf.at[x], rx_s.at[0], rx_r.at[x], me).wait_recv()

    last = xbuf[0]
    for s in range(1, N):
        last = last + xbuf[s]
    for r in range(3):
        weight_grad[r * 8 : r * 8 + 8, :] = last[:, r * 64 : r * 64 + 48] * (1.0 / 1024)

    for c in z_copies + y_copies + ry_copies:
        c.wait_send()

    @pl.when(taker != core)
    def _():
        for p in range(2):
            y_copy(p, 0).wait_send()

    for i in range(4):
        for cc in range(2):
            @pl.when(jnp.logical_not(stays(i, cc)))
            def _():
                rx_copy(i, cc).wait_send()

    for c in list(pair.values()) + list(ring.values()) + list(gather.values()):
        c.wait_send()
    for way, s, q in forward:
        shared(way, s, q, core).wait_send()


def store(encoded, ctx_grad, weight_grad, encoded_hbm, ctx_grad_hbm, weight_grad_hbm, sems):
    copies = [pltpu.make_async_copy(weight_grad, weight_grad_hbm, sems.at[2, 0])]
    rows = encoded.shape[0] // PIECES
    for i in range(PIECES):
        spot = slice(i * rows, (i + 1) * rows)
        copies.append(pltpu.make_async_copy(encoded.at[spot], encoded_hbm.at[spot], sems.at[0, i]))
        copies.append(pltpu.make_async_copy(ctx_grad.at[spot], ctx_grad_hbm.at[spot], sems.at[1, i]))
    for c in copies:
        c.start()
    for c in copies:
        c.wait()


def body(context, cotangent, codes, scales, lengths):
    frames, hrows = context.shape
    width = cotangent.shape[1]
    vmem = pl.BlockSpec(memory_space=pltpu.VMEM)
    hbm = pl.BlockSpec(memory_space=pltpu.HBM)
    dma = pltpu.SemaphoreType.DMA
    shape = jax.ShapeDtypeStruct
    operands = [
        pltpu.with_memory_space_constraint(a, pltpu.HBM)
        for a in (context, cotangent, codes, scales.T)
    ]
    held = pl.pallas_call(
        kernel,
        out_shape=(
            pltpu.VMEM((frames, width), BF16), pltpu.VMEM((frames, hrows), BF16),
            pltpu.VMEM(codes.shape, F32),
        ),
        in_specs=[hbm] * 5,
        out_specs=(vmem, vmem, vmem),
        scratch_shapes=[
            pltpu.VMEM((frames, hrows), BF16),
            pltpu.VMEM((frames, width), BF16),
            pltpu.VMEM(codes.shape, BF16),
            pltpu.VMEM((1, codes.shape[0]), BF16),
            pltpu.SMEM((1, 1), jnp.int32),
            pltpu.VMEM((hrows, frames), BF16),
            pltpu.VMEM((4, frames, hrows // 4), BF16),
            pltpu.VMEM((2, frames, width // 2), BF16),
            pltpu.VMEM((2, frames, width // 2), F32),
            pltpu.VMEM((4, frames, hrows // 4), F32),
            pltpu.VMEM((2, 4, N, 24, width // 2), F32),
            pltpu.VMEM((N, 4, 24, width // 2), F32),
            pltpu.VMEM((hrows, width), BF16),
            pltpu.VMEM((192, 384), F32),
            pltpu.VMEM((32, 128), BF16),
            pltpu.VMEM((N, 32, 128), BF16),
            pltpu.VMEM((96, 128), F32),
            pltpu.VMEM((96, 128), BF16),
            pltpu.VMEM((N, 96, 128), BF16),
            pltpu.VMEM((2, 5, 4, 48, 384), BF16),
            pltpu.VMEM((2, 5, 4, 48, 384), BF16),
            pltpu.VMEM((N, 96, 128), BF16),
            pltpu.VMEM((N, 96, 128), BF16),
            pltpu.VMEM((4, 2, 8, 256), F32),
            pltpu.VMEM((N, 8, 256), F32),
            dma((3, PIECES)),
            dma((N,)), dma((N,)),
            dma((2, N)), dma((2, N)),
            dma((2, 5, 4)), dma((2, 5, 4)),
            dma((2, 5, 4)), dma((2, 5, 4)),
            dma((N,)), dma((N,)),
            dma((2, 5, 4)), dma((2, 5, 4)),
            dma((2, N)), dma((2, N)),
            dma((N,)), dma((N,)),
        ],
        compiler_params=pltpu.CompilerParams(
            collective_id=0, has_side_effects=True, vmem_limit_bytes=40 * 2**20
        ),
    )(*operands, lengths.reshape(1, 1))
    return pl.pallas_call(
        store,
        out_shape=(
            shape((frames, width), BF16), shape((frames, hrows), BF16), shape(codes.shape, F32),
        ),
        in_specs=[vmem] * 3,
        out_specs=(hbm,) * 3,
        scratch_shapes=[dma((3, PIECES))],
    )(*(pltpu.with_memory_space_constraint(a, pltpu.VMEM) for a in held))


def solution(mesh):
    return jax.shard_map(
        body,
        mesh=mesh,
        in_specs=(
            P(("node", "local"), None),
            P(("node", "local"), None),
            P("local", "node"),
            P("local", "node"),
            P(("node", "local")),
        ),
        out_specs=(P(("node", "local"), None), P(("node", "local"), None), P("local", "node")),
        check_vma=False,
    )
```
